32 devices in a mesh: grp: 1, tm: 8 (over y, x, core), op: 4 (over z).
Axes of the slice: x: 2, y: 2, z: 4, core: 2. Of those that a mesh axis runs over, the one named last changes fastest.
Arguments:
- sources: bfloat16 [8, 16, 2, 384, 384], P(('grp', 'tm'), 'op'), may hold values from -6 to 6
- sink: bfloat16 [8, 2, 384, 384], P(('grp', 'tm')), may hold values from -0.3125 to 0.3125
- phase: float32 [8, 384], replicated, may hold values from -3.140625 to 3.140625
- task_table: int32 [3, 8, 16], P(None, ('grp', 'tm'), 'op'), may hold values from -1 to 15, as said below
Outputs:
- task_values: float32 [8, 16, 2, 384], P(('grp', 'tm'), 'op')
The draws below stay inside these ranges and needn't reach their ends.
Inputs may be any that keep to these rules, and one draw needn't show every extreme that they name: `task_table`: field 0 lies in 0 to 15, field 1 in 0 to 7, field 2 is -1 (dead slot) or a rank 0 to 1. At each time slice, for every owner s exactly 2 homes have slot s live, and their places are 0 to 1, each once. At each time slice one home has all 4 slots live.
All inputs are finite; a program needn't handle non-finite values.
Results may differ from the reference program's by a relative error of at most 0.004.
Values may be sent and summed in bfloat16 or wider, within the bound.
A program may use at most 64 MiB of HBM per device.

```python
import jax
import jax.numpy as jnp
from jax import lax

DIM = 384
OPS_DEV = 4
MOMENTA = 8
CAPACITY = 2
TIMES = 8
OPERATORS = 16
TASKS_DEV = 4


def draw_task_table(key, part):
    homes = TASKS_DEV
    slots = TASKS_DEV
    picks = jax.random.randint(jax.random.fold_in(key, 11), (TIMES, homes * slots), 0, 4 * OPS_DEV)
    moments = jax.random.randint(jax.random.fold_in(key, 12), (TIMES, homes * slots), 0, MOMENTA)
    fullest = jax.random.randint(jax.random.fold_in(key, 13), (TIMES,), 0, homes)
    scores = jax.random.randint(jax.random.fold_in(key, 14), (TIMES, slots, homes), 0, 1048576)
    home_ids = jnp.arange(homes, dtype=jnp.int32)
    scores = jnp.where(home_ids[None, None, :] == fullest[:, None, None], -1, scores)
    keyed = scores * homes + home_ids[None, None, :]
    order = jnp.argsort(keyed, axis=-1)
    ranks = jnp.argsort(order, axis=-1)
    places = jnp.where(ranks < CAPACITY, ranks, -1)
    places = jnp.transpose(places, (0, 2, 1)).reshape(TIMES, homes * slots)
    return jnp.stack([picks, moments, places]).astype(jnp.int32)


def shard_levels(own_key, extent, pieces, least, top_value):
    def one(position, shards_of):
        steps = jax.random.uniform(jax.random.fold_in(jax.random.fold_in(own_key, 6), position), (shards_of,), jnp.float32, least / len(pieces), top_value / len(pieces))
        return jnp.repeat(jnp.exp(steps), extent[position] // shards_of).reshape((-1,) + (1,) * (len(extent) - position - 1))

    gain = one(*pieces[0])
    for cut in pieces[1:]:
        gain = gain * one(*cut)
    return gain


def noise(own_key, shape, scale, bound, pieces=(), kind=jnp.bfloat16):
    result = scale * jax.random.normal(own_key, shape, jnp.float32)
    if pieces:
        result = result * shard_levels(own_key, shape, pieces, -0.22, 0.18)
    return jnp.clip(result, -bound, bound).astype(kind)


def setup_inputs(seed: int = 0, part: int = 0) -> dict:
    splits = jax.random.split(jax.random.key(seed), 5)
    part_splits = jax.random.split(jax.random.fold_in(splits[4], part), 5)
    return {
        "sources": noise(part_splits[0], (TIMES, OPERATORS, 2, DIM, DIM), 1.0, 6.0, ((0, 8), (1, 4))),
        "sink": noise(part_splits[1], (TIMES, 2, DIM, DIM), DIM ** -0.5, 0.3125, ((0, 8),)),
        "phase": jnp.clip(jax.random.uniform(splits[2], (MOMENTA, DIM), jnp.float32, -3.140625, 3.140625), -3.140625, 3.140625),
        "task_table": draw_task_table(jax.random.fold_in(jax.random.fold_in(splits[4], part), 71), part),
    }


SEPARATIONS = (-2, -1, 1, 2)


def task_value(source, angle, sink_slice):
    highest = lax.Precision.HIGHEST
    sink_wide = sink_slice.astype(jnp.float32)
    blocks = jnp.einsum("xij,yjl->xyil", source.astype(jnp.float32), sink_wide, precision=highest)
    quark_real = blocks[0, 0] - blocks[1, 1]
    quark_imag = blocks[0, 1] + blocks[1, 0]
    cosine = jnp.cos(angle)[None, :]
    sine = jnp.sin(angle)[None, :]
    phased = jnp.stack([quark_real * cosine - quark_imag * sine, quark_real * sine + quark_imag * cosine])
    phased = phased.astype(jnp.bfloat16).astype(jnp.float32)
    second = jnp.einsum("xil,yjl->xyij", phased, sink_wide, precision=highest)
    loop_real = second[0, 0] + second[1, 1]
    loop_imag = second[1, 0] - second[0, 1]
    diag_real = jnp.sum(loop_real * loop_real.T - loop_imag * loop_imag.T, axis=1)
    diag_imag = jnp.sum(loop_real * loop_imag.T + loop_imag * loop_real.T, axis=1)
    return jnp.stack([diag_real, diag_imag]) / loop_real.shape[0]


def reference(sources, sink, phase, task_table):
    slots = task_table.shape[2]
    offsets = jnp.array(SEPARATIONS, dtype=jnp.int32)

    def one_task(index):
        time_index = index // slots
        slot = index % slots
        pick = task_table[0, time_index, slot]
        moment = task_table[1, time_index, slot]
        place = task_table[2, time_index, slot]
        home = slot // TASKS_DEV
        source_time = (time_index + offsets[pick // OPS_DEV] + TIMES) % TIMES
        operator = home * OPS_DEV + pick % OPS_DEV
        value = task_value(sources[source_time, operator], phase[moment], sink[time_index])
        return value * (place >= 0).astype(jnp.float32)

    values = lax.map(one_task, jnp.arange(TIMES * slots, dtype=jnp.int32))
    return values.reshape(TIMES, slots, 2, values.shape[-1])
```

```python
import functools

import jax
import jax.numpy as jnp
from jax import lax
from jax.experimental import pallas as pl
from jax.experimental.pallas import tpu as pltpu
from jax.sharding import PartitionSpec as P

SEPARATIONS = (-2, -1, 1, 2)
MESH = pl.DeviceIdType.MESH


def greet(neighbours):
    barrier = pltpu.get_barrier_semaphore()
    for neighbour in neighbours:
        pl.semaphore_signal(barrier, inc=1, device_id={"tm": neighbour}, device_id_type=MESH)
    pl.semaphore_wait(barrier, len(neighbours))


def remote(src, dst, send, recv, neighbour):
    return pltpu.make_async_remote_copy(
        src_ref=src, dst_ref=dst, send_sem=send, recv_sem=recv,
        device_id={"tm": neighbour}, device_id_type=MESH,
    )


def gather_kernel(
    n, pieces, table_ref, sink_ref, sinks_ref, tables_ref,
    own, t_send, t_recv, x_send, x_recv, y_send, y_recv, p_send, p_recv, f_send, f_recv,
):
    me = lax.axis_index("tm")
    slots = table_ref.shape[2]
    chip, core = me // 2, me % 2
    mate = chip * 2 + 1 - core
    relay = n == 8
    neighbours = [(me - d + n) % n for d in SEPARATIONS]
    if relay:
        across = ((chip // 2) * 2 + 1 - chip % 2) * 2 + core
        beside = (me + n // 2) % n
        greet(neighbours + [beside])
    else:
        greet(neighbours)

    rows = sink_ref.shape[0] // pieces

    def part(ref, k):
        return ref.at[pl.ds(k * rows, rows)]

    if relay:
        x_here = 3 * (chip % 2)
        y_here = 3 - x_here
        x_copies = [
            remote(part(sink_ref, k), part(sinks_ref.at[3 - x_here], k), x_send.at[k], x_recv.at[k], across)
            for k in range(pieces)
        ]
        y_copies = [
            remote(part(sinks_ref.at[x_here], k), part(sinks_ref.at[y_here], k), y_send.at[k], y_recv.at[k], beside)
            for k in range(pieces)
        ]
    else:
        x_copies = [
            remote(part(sink_ref, k), part(sinks_ref.at[0], k), x_send.at[k], x_recv.at[k], (me + n - 2) % n)
            for k in range(pieces)
        ]
        y_copies = [
            remote(part(sink_ref, k), part(sinks_ref.at[3], k), y_send.at[k], y_recv.at[k], (me + 2) % n)
            for k in range(pieces)
        ]
    p_copy = remote(sink_ref, sinks_ref.at[2 - core], p_send, p_recv, mate)
    f_copies = [
        remote(part(sinks_ref.at[3 * core], k), part(sinks_ref.at[1 + core], k), f_send.at[k], f_recv.at[k], mate)
        for k in range(pieces)
    ]

    for copy in x_copies:
        copy.start()
    if not relay:
        for copy in y_copies:
            copy.start()
    p_copy.start()

    row = lax.broadcasted_iota(jnp.int32, own.shape, 0)
    lane = lax.broadcasted_iota(jnp.int32, own.shape, 1)
    packed = jnp.zeros(own.shape, jnp.int32)
    for f in range(3):
        for s in range(slots):
            packed = jnp.where((row == f) & (lane == s), table_ref[f, 0, s], packed)
    own[...] = packed
    t_copies = [
        remote(own, tables_ref.at[o], t_send.at[o], t_recv.at[o], (me + d + n) % n)
        for o, d in enumerate(SEPARATIONS)
    ]
    for copy in t_copies:
        copy.start()

    for k in range(pieces):
        x_copies[k].wait_recv()
        if relay:
            y_copies[k].start()

            @pl.when(3 * core == x_here)
            def _():
                f_copies[k].start()
        else:
            @pl.when(core == 0)
            def _():
                f_copies[k].start()
    for k in range(pieces):
        y_copies[k].wait_recv()
        if relay:
            @pl.when(3 * core != x_here)
            def _():
                f_copies[k].start()
        else:
            @pl.when(core == 1)
            def _():
                f_copies[k].start()
    for copy in t_copies:
        copy.wait()
    p_copy.wait()
    for k in range(pieces):
        f_copies[k].wait()
        x_copies[k].wait_send()
        y_copies[k].wait_send()


def task_kernel(
    tables_ref, phase_ref, sources_ref, sinks_ref, out_ref, source, weight, cosine, sine, todo, sems,
):
    offsets, slots = out_ref.shape[:2]
    ops, dim = sources_ref.shape[0], source.shape[1]

    def scan(j, count):
        o, s = j // slots, j % slots
        mine = (tables_ref[o, 2, s] >= 0) & (tables_ref[o, 0, s] // ops == o)

        @pl.when(mine)
        def _():
            todo[count] = j

        return count + mine.astype(jnp.int32)

    count = lax.fori_loop(0, offsets * slots, scan, jnp.int32(0))

    def copies(i):
        j, slot = todo[i], i % 2
        o, s = j // slots, j % slots
        a = tables_ref[o, 0, s] % ops
        first, last = pl.ds(0, dim), pl.ds(dim, dim)
        pairs = (
            (sources_ref.at[a, 0], source.at[slot, :, first]),
            (sources_ref.at[a, 1], source.at[slot, :, last]),
            (sinks_ref.at[o, 0], weight.at[slot, first, first]),
            (sinks_ref.at[o, 0], weight.at[slot, last, last]),
            (sinks_ref.at[o, 1], weight.at[slot, first, last]),
        )
        return [pltpu.make_async_copy(a, b, sems.at[slot, q]) for q, (a, b) in enumerate(pairs)]

    @pl.when(count > 0)
    def _():
        for copy in copies(0):
            copy.start()

    out_ref[...] = jnp.zeros_like(out_ref)
    cosine[...] = jnp.cos(phase_ref[...])
    sine[...] = jnp.sin(phase_ref[...])

    def step(i, carry):
        slot = i % 2
        for copy in copies(i):
            copy.wait()

        @pl.when(i + 1 < count)
        def _():
            for copy in copies(i + 1):
                copy.start()

        j = todo[i]
        o, s = j // slots, j % slots
        moment = tables_ref[o, 1, s]
        weight[slot, dim:, :dim] = -weight[slot, :dim, dim:]
        quark = jnp.dot(source[slot], weight[slot], preferred_element_type=jnp.float32)
        c, z = cosine[pl.ds(moment, 1), :], sine[pl.ds(moment, 1), :]
        real, imag = quark[:, :dim], quark[:, dim:]
        phased = jnp.concatenate([real * c - imag * z, real * z + imag * c], axis=1).astype(jnp.bfloat16)
        loop = lax.dot_general(
            phased, weight[slot], (((1,), (1,)), ((), ())), preferred_element_type=jnp.float32
        )
        real, imag = loop[:, :dim], loop[:, dim:]
        real_t, imag_t = real.T, imag.T
        out_ref[o, s, 0:1] = jnp.sum(real * real_t - imag * imag_t, axis=0, keepdims=True) / dim
        out_ref[o, s, 1:2] = jnp.sum(real * imag_t + imag * real_t, axis=0, keepdims=True) / dim
        return carry

    lax.fori_loop(0, count, step, 0)


def return_kernel(n, values_ref, out_ref, parts, send, recv):
    me = lax.axis_index("tm")
    owners = [(me - d + n) % n for d in SEPARATIONS]
    greet(owners)
    copies = [
        remote(values_ref.at[o], parts.at[o], send.at[o], recv.at[o], owner) for o, owner in enumerate(owners)
    ]
    for copy in copies:
        copy.start()
    for copy in copies:
        copy.wait()
    out_ref[0] = (parts[0] + parts[1]) + (parts[2] + parts[3])


def shards(n, sources, sink, phase, task_table):
    ops, dim = sources.shape[1], sources.shape[-1]
    slots = task_table.shape[2]
    offsets = len(SEPARATIONS)
    pieces = 8 if (2 * dim) % 128 == 0 else 1
    any_spec = pl.BlockSpec(memory_space=pl.ANY)
    smem_spec = pl.BlockSpec(memory_space=pltpu.SMEM)
    vmem_spec = pl.BlockSpec(memory_space=pltpu.VMEM)
    dma = pltpu.SemaphoreType.DMA
    sinks, tables = pl.pallas_call(
        functools.partial(gather_kernel, n, pieces),
        out_shape=(
            jax.ShapeDtypeStruct((offsets, 2 * dim, dim), sink.dtype),
            jax.ShapeDtypeStruct((offsets, 8, 128), jnp.int32),
        ),
        in_specs=[smem_spec, any_spec],
        out_specs=(any_spec, any_spec),
        scratch_shapes=[
            pltpu.VMEM((8, 128), jnp.int32),
            dma((offsets,)), dma((offsets,)),
            dma((pieces,)), dma((pieces,)), dma((pieces,)), dma((pieces,)),
            dma, dma, dma((pieces,)), dma((pieces,)),
        ],
        compiler_params=pltpu.CompilerParams(collective_id=0, has_side_effects=True),
        name="gather_sinks",
    )(task_table, sink.reshape(2 * dim, dim))
    values = pl.pallas_call(
        task_kernel,
        out_shape=jax.ShapeDtypeStruct((offsets, slots, 2, dim), jnp.float32),
        in_specs=[smem_spec, vmem_spec, any_spec, any_spec],
        out_specs=vmem_spec,
        scratch_shapes=[
            pltpu.VMEM((2, dim, 2 * dim), sources.dtype),
            pltpu.VMEM((2, 2 * dim, 2 * dim), sources.dtype),
            pltpu.VMEM(phase.shape, jnp.float32),
            pltpu.VMEM(phase.shape, jnp.float32),
            pltpu.SMEM((offsets * slots,), jnp.int32),
            dma((2, 5)),
        ],
        compiler_params=pltpu.CompilerParams(vmem_limit_bytes=40 * 1024 * 1024),
        name="tasks",
    )(tables, phase, sources[0], sinks.reshape(offsets, 2, dim, dim))
    return pl.pallas_call(
        functools.partial(return_kernel, n),
        out_shape=jax.ShapeDtypeStruct((1, slots, 2, dim), jnp.float32),
        in_specs=[vmem_spec],
        out_specs=vmem_spec,
        scratch_shapes=[
            pltpu.VMEM((offsets, slots, 2, dim), jnp.float32),
            dma((offsets,)), dma((offsets,)),
        ],
        compiler_params=pltpu.CompilerParams(collective_id=1, has_side_effects=True),
        name="return_values",
    )(values)


def solution(mesh):
    return jax.shard_map(
        functools.partial(shards, mesh.shape["tm"]),
        mesh=mesh,
        in_specs=(
            P(("grp", "tm"), "op", None, None, None),
            P(("grp", "tm"), None, None, None),
            P(),
            P(None, ("grp", "tm"), "op"),
        ),
        out_specs=P(("grp", "tm"), "op", None, None),
        check_vma=False,
    )
```

```python
import functools

import jax
import jax.numpy as jnp
from jax import lax
from jax.experimental import pallas as pl
from jax.experimental.pallas import tpu as pltpu
from jax.sharding import PartitionSpec as P

SEPARATIONS = (-2, -1, 1, 2)
MESH = pl.DeviceIdType.MESH


def greet(neighbours):
    barrier = pltpu.get_barrier_semaphore()
    for neighbour in neighbours:
        pl.semaphore_signal(barrier, inc=1, device_id=neighbour, device_id_type=MESH)
    pl.semaphore_wait(barrier, len(neighbours))


def remote(src, dst, send, recv, neighbour):
    return pltpu.make_async_remote_copy(
        src_ref=src, dst_ref=dst, send_sem=send, recv_sem=recv,
        device_id=neighbour, device_id_type=MESH,
    )


def relays(n, layers):
    return n == 8 and layers % 2 == 0


def gather_kernel(
    n, layers, third, table_ref, sink_ref, sinks_ref, tables_ref,
    own, t_send, t_recv, x_send, x_recv, y_send, y_recv, zx_send, zx_recv, zy_send, zy_recv,
    p_send, p_recv, f_send, f_recv,
):
    me = lax.axis_index("tm")
    slots = table_ref.shape[2]
    chip, core = me // 2, me % 2
    mate = {"tm": chip * 2 + 1 - core}
    relay = relays(n, layers)
    neighbours = [{"tm": (me - d + n) % n} for d in SEPARATIONS]
    rows = sink_ref.shape[0] // (3 * third)

    def part(ref, k):
        return ref.at[pl.ds(pl.multiple_of(k * rows, rows), rows)]

    if relay:
        layer = lax.axis_index("op")
        parity = layer % 2
        across = {"tm": ((chip // 2) * 2 + 1 - chip % 2) * 2 + core}
        beside = {"tm": (me + n // 2) % n}
        above = {"op": layer + 1 - 2 * parity}
        greet(neighbours + [beside, above])
        mine = [third * (1 + parity) + j for j in range(third)] + list(range(third))
        others = [third * (2 - parity) + j for j in range(third)]
        x_here = 3 * (chip % 2)
        y_here = 3 - x_here
        x_copies = [
            remote(part(sink_ref, p), part(sinks_ref.at[y_here], p), x_send.at[k], x_recv.at[k], across)
            for k, p in enumerate(mine)
        ]
        y_copies = [
            remote(part(sinks_ref.at[x_here], p), part(sinks_ref.at[y_here], p), y_send.at[k], y_recv.at[k], beside)
            for k, p in enumerate(mine)
        ]
        zx_copies = [
            remote(part(sinks_ref.at[x_here], p), part(sinks_ref.at[x_here], p), zx_send.at[k], zx_recv.at[k], above)
            for k, p in enumerate(mine[:third])
        ]
        zy_copies = [
            remote(part(sinks_ref.at[y_here], p), part(sinks_ref.at[y_here], p), zy_send.at[k], zy_recv.at[k], above)
            for k, p in enumerate(mine[:third])
        ]
        order = mine + others
        x_forward = 3 * core == x_here
    else:
        greet(neighbours)
        order = list(range(3 * third))
        x_copies = [
            remote(part(sink_ref, p), part(sinks_ref.at[0], p), x_send.at[p], x_recv.at[p], neighbours[3])
            for p in order
        ]
        y_copies = [
            remote(part(sink_ref, p), part(sinks_ref.at[3], p), y_send.at[p], y_recv.at[p], neighbours[0])
            for p in order
        ]
        x_forward = core == 0
    p_copy = remote(sink_ref, sinks_ref.at[2 - core], p_send, p_recv, mate)
    f_copies = [
        remote(part(sinks_ref.at[3 * core], p), part(sinks_ref.at[1 + core], p), f_send.at[k], f_recv.at[k], mate)
        for k, p in enumerate(order)
    ]

    def forward(k, now):
        @pl.when(now)
        def _():
            f_copies[k].start()

    for copy in x_copies:
        copy.start()
    if not relay:
        for copy in y_copies:
            copy.start()

    row = lax.broadcasted_iota(jnp.int32, own.shape, 0)
    lane = lax.broadcasted_iota(jnp.int32, own.shape, 1)
    packed = jnp.zeros(own.shape, jnp.int32)
    for f in range(3):
        for s in range(slots):
            packed = jnp.where((row == f) & (lane == s), table_ref[f, 0, s], packed)
    own[...] = packed
    t_copies = [
        remote(own, tables_ref.at[o], t_send.at[o], t_recv.at[o], {"tm": (me + d + n) % n})
        for o, d in enumerate(SEPARATIONS)
    ]
    for copy in t_copies:
        copy.start()
    p_copy.start()

    steps = len(x_copies)
    for k in range(steps + 1):
        if k < steps:
            x_copies[k].wait_recv()
            if relay:
                y_copies[k].start()
                if k < third:
                    zx_copies[k].start()
            forward(k, x_forward)
        if k > 0:
            y_copies[k - 1].wait_recv()
            if relay and k - 1 < third:
                zy_copies[k - 1].start()
            forward(k - 1, jnp.logical_not(x_forward))
        if relay and third <= k < 2 * third:
            j = k - third
            zx_copies[j].wait_recv()
            forward(steps + j, x_forward)
            zy_copies[j].wait_recv()
            forward(steps + j, jnp.logical_not(x_forward))
    for copy in t_copies:
        copy.wait()
    p_copy.wait()
    for copy in f_copies:
        copy.wait()
    for copy in x_copies + y_copies:
        copy.wait_send()
    if relay:
        for copy in zx_copies + zy_copies:
            copy.wait_send()


def task_kernel(
    offsets, slots, tables_hbm, phase_hbm, sources_ref, sinks_ref, out_ref,
    source, weight, loops, tables_ref, phase_ref, cosine, sine, todo, sems, begin,
):
    ops, dim = sources_ref.shape[0], source.shape[1]
    spare = offsets * slots
    first, last = pl.ds(0, dim), pl.ds(dim, dim)
    table_copy = pltpu.make_async_copy(tables_hbm, tables_ref, begin.at[0])
    phase_copy = pltpu.make_async_copy(phase_hbm, phase_ref, begin.at[1])
    table_copy.start()
    phase_copy.start()
    out_ref[...] = jnp.zeros_like(out_ref)
    table_copy.wait()

    def scan(j, count):
        o, s = j // slots, j % slots
        mine = (tables_ref[o, 2, s] >= 0) & (tables_ref[o, 0, s] // ops == o)
        todo[count] = j
        return count + mine.astype(jnp.int32)

    count = lax.fori_loop(0, offsets * slots, scan, jnp.int32(0))

    def copies(i):
        j, slot = todo[i], i % 2
        o, s = j // slots, j % slots
        a = tables_ref[o, 0, s] % ops
        pairs = (
            (sources_ref.at[a, 0], source.at[slot, :, first]),
            (sources_ref.at[a, 1], source.at[slot, :, last]),
            (sinks_ref.at[o, 0], weight.at[slot, first, first]),
            (sinks_ref.at[o, 0], weight.at[slot, last, last]),
            (sinks_ref.at[o, 1], weight.at[slot, first, last]),
        )
        return [pltpu.make_async_copy(a, b, sems.at[slot, q]) for q, (a, b) in enumerate(pairs)]

    @pl.when(count > 0)
    def _():
        for copy in copies(0):
            copy.start()

    phase_copy.wait()
    cosine[...] = jnp.cos(phase_ref[...])
    sine[...] = jnp.sin(phase_ref[...])

    def finish(slot, j):
        real, imag = loops[slot, :, :dim], loops[slot, :, dim:]
        real_t, imag_t = real.T, imag.T
        out_ref[j, 0:1] = jnp.sum(real * real_t - imag * imag_t, axis=0, keepdims=True) / dim
        out_ref[j, 1:2] = jnp.sum(real * imag_t + imag * real_t, axis=0, keepdims=True) / dim

    def step(i, before):
        slot = i % 2
        for copy in copies(i):
            copy.wait()

        @pl.when(i + 1 < count)
        def _():
            for copy in copies(i + 1):
                copy.start()

        j = todo[i]
        moment = tables_ref[j // slots, 1, j % slots]
        weight[slot, dim:, :dim] = -weight[slot, :dim, dim:]
        quark = jnp.dot(source[slot], weight[slot], preferred_element_type=jnp.float32)
        finish(1 - slot, before)
        c, z = cosine[pl.ds(moment, 1), :], sine[pl.ds(moment, 1), :]
        real, imag = quark[:, :dim], quark[:, dim:]
        phased = jnp.concatenate([real * c - imag * z, real * z + imag * c], axis=1).astype(jnp.bfloat16)
        loops[slot] = lax.dot_general(
            phased, weight[slot], (((1,), (1,)), ((), ())), preferred_element_type=jnp.float32
        )
        return j

    final = lax.fori_loop(0, count, step, jnp.int32(spare))

    @pl.when(count > 0)
    def _():
        finish((count - 1) % 2, final)


def return_kernel(n, values_ref, out_ref, parts, send, recv):
    me = lax.axis_index("tm")
    slots = out_ref.shape[1]
    owners = [{"tm": (me - d + n) % n} for d in SEPARATIONS]
    greet(owners)
    copies = [
        remote(values_ref.at[pl.ds(o * slots, slots)], parts.at[o], send.at[o], recv.at[o], owner)
        for o, owner in enumerate(owners)
    ]
    for copy in copies:
        copy.start()
    for copy in copies:
        copy.wait()
    out_ref[0] = (parts[0] + parts[1]) + (parts[2] + parts[3])


def shards(n, layers, sources, sink, phase, task_table):
    ops, dim = sources.shape[1], sources.shape[-1]
    slots = task_table.shape[2]
    offsets = len(SEPARATIONS)
    third = 4
    steps = 2 * third if relays(n, layers) else 3 * third
    any_spec = pl.BlockSpec(memory_space=pl.ANY)
    smem_spec = pl.BlockSpec(memory_space=pltpu.SMEM)
    vmem_spec = pl.BlockSpec(memory_space=pltpu.VMEM)
    dma = pltpu.SemaphoreType.DMA
    limit = 60 * 1024 * 1024
    sinks, tables = pl.pallas_call(
        functools.partial(gather_kernel, n, layers, third),
        out_shape=(
            jax.ShapeDtypeStruct((offsets, 2 * dim, dim), sink.dtype),
            jax.ShapeDtypeStruct((offsets, 8, 128), jnp.int32),
        ),
        in_specs=[smem_spec, any_spec],
        out_specs=(any_spec, any_spec),
        scratch_shapes=[
            pltpu.VMEM((8, 128), jnp.int32),
            dma((offsets,)), dma((offsets,)),
            dma((steps,)), dma((steps,)), dma((steps,)), dma((steps,)),
            dma((third,)), dma((third,)), dma((third,)), dma((third,)),
            dma, dma, dma((3 * third,)), dma((3 * third,)),
        ],
        compiler_params=pltpu.CompilerParams(collective_id=0, has_side_effects=True, vmem_limit_bytes=limit),
        name="gather_sinks",
    )(task_table, sink.reshape(2 * dim, dim))
    values = pl.pallas_call(
        functools.partial(task_kernel, offsets, slots),
        out_shape=jax.ShapeDtypeStruct((offsets * slots + 1, 2, dim), jnp.float32),
        in_specs=[any_spec] * 4,
        out_specs=vmem_spec,
        scratch_shapes=[
            pltpu.VMEM((2, dim, 2 * dim), sources.dtype),
            pltpu.VMEM((2, 2 * dim, 2 * dim), sources.dtype),
            pltpu.VMEM((2, dim, 2 * dim), jnp.float32),
            pltpu.SMEM((offsets, 8, 128), jnp.int32),
            pltpu.VMEM(phase.shape, jnp.float32),
            pltpu.VMEM(phase.shape, jnp.float32),
            pltpu.VMEM(phase.shape, jnp.float32),
            pltpu.SMEM((offsets * slots,), jnp.int32),
            dma((2, 5)), dma((2,)),
        ],
        compiler_params=pltpu.CompilerParams(vmem_limit_bytes=limit),
        name="tasks",
    )(tables, phase, sources[0], sinks.reshape(offsets, 2, dim, dim))
    return pl.pallas_call(
        functools.partial(return_kernel, n),
        out_shape=jax.ShapeDtypeStruct((1, slots, 2, dim), jnp.float32),
        in_specs=[any_spec],
        out_specs=vmem_spec,
        scratch_shapes=[
            pltpu.VMEM((offsets, slots, 2, dim), jnp.float32),
            dma((offsets,)), dma((offsets,)),
        ],
        compiler_params=pltpu.CompilerParams(collective_id=1, has_side_effects=True, vmem_limit_bytes=limit),
        name="return_values",
    )(values)


def solution(mesh):
    return jax.shard_map(
        functools.partial(shards, mesh.shape["tm"], mesh.shape["op"]),
        mesh=mesh,
        in_specs=(
            P(("grp", "tm"), "op", None, None, None),
            P(("grp", "tm"), None, None, None),
            P(),
            P(None, ("grp", "tm"), "op"),
        ),
        out_specs=P(("grp", "tm"), "op", None, None),
        check_vma=False,
    )
```

```python
import functools

import jax
import jax.numpy as jnp
from jax import lax
from jax.experimental import pallas as pl
from jax.experimental.pallas import tpu as pltpu
from jax.sharding import PartitionSpec as P

SEPARATIONS = (-2, -1, 1, 2)
MESH = pl.DeviceIdType.MESH


def greet(neighbours):
    barrier = pltpu.get_barrier_semaphore()
    for neighbour in neighbours:
        pl.semaphore_signal(barrier, inc=1, device_id=neighbour, device_id_type=MESH)
    pl.semaphore_wait(barrier, len(neighbours))


def remote(src, dst, send, recv, neighbour):
    return pltpu.make_async_remote_copy(
        src_ref=src, dst_ref=dst, send_sem=send, recv_sem=recv,
        device_id=neighbour, device_id_type=MESH,
    )


def relays(n, layers):
    return n == 8 and layers % 2 == 0


def gather_kernel(
    n, layers, third, table_ref, sink_ref, sinks_ref, tables_ref,
    own, t_send, t_recv, x_send, x_recv, y_send, y_recv, zx_send, zx_recv, zy_send, zy_recv,
    p_send, p_recv, f_send, f_recv,
):
    me = lax.axis_index("tm")
    slots = table_ref.shape[2]
    chip, core = me // 2, me % 2
    mate = {"tm": chip * 2 + 1 - core}
    relay = relays(n, layers)
    neighbours = [{"tm": (me - d + n) % n} for d in SEPARATIONS]
    rows = sink_ref.shape[0] // (3 * third)

    def part(ref, k):
        return ref.at[pl.ds(pl.multiple_of(k * rows, rows), rows)]

    if relay:
        layer = lax.axis_index("op")
        parity = layer % 2
        across = {"tm": ((chip // 2) * 2 + 1 - chip % 2) * 2 + core}
        beside = {"tm": (me + n // 2) % n}
        above = {"op": layer + 1 - 2 * parity}
        greet(neighbours + [beside, above])
        mine = [third * (1 + parity) + j for j in range(third)] + list(range(third))
        others = [third * (2 - parity) + j for j in range(third)]
        x_here = 3 * (chip % 2)
        y_here = 3 - x_here
        x_copies = [
            remote(part(sink_ref, p), part(sinks_ref.at[y_here], p), x_send.at[k], x_recv.at[k], across)
            for k, p in enumerate(mine)
        ]
        y_copies = [
            remote(part(sinks_ref.at[x_here], p), part(sinks_ref.at[y_here], p), y_send.at[k], y_recv.at[k], beside)
            for k, p in enumerate(mine)
        ]
        zx_copies = [
            remote(part(sinks_ref.at[x_here], p), part(sinks_ref.at[x_here], p), zx_send.at[k], zx_recv.at[k], above)
            for k, p in enumerate(mine[:third])
        ]
        zy_copies = [
            remote(part(sinks_ref.at[y_here], p), part(sinks_ref.at[y_here], p), zy_send.at[k], zy_recv.at[k], above)
            for k, p in enumerate(mine[:third])
        ]
        order = mine + others
        x_forward = 3 * core == x_here
    else:
        greet(neighbours)
        order = list(range(3 * third))
        x_copies = [
            remote(part(sink_ref, p), part(sinks_ref.at[0], p), x_send.at[p], x_recv.at[p], neighbours[3])
            for p in order
        ]
        y_copies = [
            remote(part(sink_ref, p), part(sinks_ref.at[3], p), y_send.at[p], y_recv.at[p], neighbours[0])
            for p in order
        ]
        x_forward = core == 0
    p_copy = remote(sink_ref, sinks_ref.at[2 - core], p_send, p_recv, mate)
    f_copies = [
        remote(part(sinks_ref.at[3 * core], p), part(sinks_ref.at[1 + core], p), f_send.at[k], f_recv.at[k], mate)
        for k, p in enumerate(order)
    ]

    def forward(k, now):
        @pl.when(now)
        def _():
            f_copies[k].start()

    for copy in x_copies:
        copy.start()
    if not relay:
        for copy in y_copies:
            copy.start()

    row = lax.broadcasted_iota(jnp.int32, own.shape, 0)
    lane = lax.broadcasted_iota(jnp.int32, own.shape, 1)
    packed = jnp.zeros(own.shape, jnp.int32)
    for f in range(3):
        for s in range(slots):
            packed = jnp.where((row == f) & (lane == s), table_ref[f, 0, s], packed)
    own[...] = packed
    t_copies = [
        remote(own, tables_ref.at[o], t_send.at[o], t_recv.at[o], {"tm": (me + d + n) % n})
        for o, d in enumerate(SEPARATIONS)
    ]
    for copy in t_copies:
        copy.start()
    p_copy.start()

    steps, lag = len(x_copies), 3
    for k in range(steps + 2 * lag):
        if k < steps:
            x_copies[k].wait_recv()
            if relay:
                y_copies[k].start()
                if k < third:
                    zx_copies[k].start()
            forward(k, x_forward)
        if 0 <= k - lag < steps:
            y_copies[k - lag].wait_recv()
            if relay and k - lag < third:
                zy_copies[k - lag].start()
            forward(k - lag, jnp.logical_not(x_forward))
        if relay and 0 <= k - third < third:
            zx_copies[k - third].wait_recv()
            forward(steps + k - third, x_forward)
        if relay and 0 <= k - 2 * lag < third:
            zy_copies[k - 2 * lag].wait_recv()
            forward(steps + k - 2 * lag, jnp.logical_not(x_forward))
    for copy in t_copies:
        copy.wait()
    p_copy.wait()
    for copy in f_copies:
        copy.wait()
    for copy in x_copies + y_copies:
        copy.wait_send()
    if relay:
        for copy in zx_copies + zy_copies:
            copy.wait_send()


def task_kernel(
    offsets, slots, tables_hbm, phase_hbm, sources_ref, sinks_ref, out_ref,
    source, weight, loops, tables_ref, phase_ref, cosine, sine, todo, sems, begin,
):
    ops, dim = sources_ref.shape[0], source.shape[1]
    spare = offsets * slots
    first, last = pl.ds(0, dim), pl.ds(dim, dim)
    table_copy = pltpu.make_async_copy(tables_hbm, tables_ref, begin.at[0])
    phase_copy = pltpu.make_async_copy(phase_hbm, phase_ref, begin.at[1])
    table_copy.start()
    phase_copy.start()
    out_ref[...] = jnp.zeros_like(out_ref)
    table_copy.wait()

    def scan(j, count):
        o, s = j // slots, j % slots
        mine = (tables_ref[o, 2, s] >= 0) & (tables_ref[o, 0, s] // ops == o)
        todo[count] = j
        return count + mine.astype(jnp.int32)

    count = lax.fori_loop(0, offsets * slots, scan, jnp.int32(0))

    def copies(i):
        j, slot = todo[i], i % 2
        o, s = j // slots, j % slots
        a = tables_ref[o, 0, s] % ops
        pairs = (
            (sources_ref.at[a, 0], source.at[slot, :, first]),
            (sources_ref.at[a, 1], source.at[slot, :, last]),
            (sinks_ref.at[o, 0], weight.at[slot, first, first]),
            (sinks_ref.at[o, 0], weight.at[slot, last, last]),
            (sinks_ref.at[o, 1], weight.at[slot, first, last]),
        )
        return [pltpu.make_async_copy(a, b, sems.at[slot, q]) for q, (a, b) in enumerate(pairs)]

    @pl.when(count > 0)
    def _():
        for copy in copies(0):
            copy.start()

    phase_copy.wait()
    cosine[...] = jnp.cos(phase_ref[...])
    sine[...] = jnp.sin(phase_ref[...])

    def finish(slot, j):
        real, imag = loops[slot, :, :dim], loops[slot, :, dim:]
        real_t, imag_t = real.T, imag.T
        out_ref[j, 0:1] = jnp.sum(real * real_t - imag * imag_t, axis=0, keepdims=True) / dim
        out_ref[j, 1:2] = jnp.sum(real * imag_t + imag * real_t, axis=0, keepdims=True) / dim

    def step(i, before):
        slot = i % 2
        for copy in copies(i):
            copy.wait()

        @pl.when(i + 1 < count)
        def _():
            for copy in copies(i + 1):
                copy.start()

        j = todo[i]
        moment = tables_ref[j // slots, 1, j % slots]
        weight[slot, dim:, :dim] = -weight[slot, :dim, dim:]
        quark = jnp.dot(source[slot], weight[slot], preferred_element_type=jnp.float32)
        finish(1 - slot, before)
        c, z = cosine[pl.ds(moment, 1), :], sine[pl.ds(moment, 1), :]
        real, imag = quark[:, :dim], quark[:, dim:]
        phased = jnp.concatenate([real * c - imag * z, real * z + imag * c], axis=1).astype(jnp.bfloat16)
        loops[slot] = lax.dot_general(
            phased, weight[slot], (((1,), (1,)), ((), ())), preferred_element_type=jnp.float32
        )
        return j

    final = lax.fori_loop(0, count, step, jnp.int32(spare))

    @pl.when(count > 0)
    def _():
        finish((count - 1) % 2, final)


def return_kernel(n, values_ref, out_ref, parts, send, recv):
    me = lax.axis_index("tm")
    slots = out_ref.shape[1]
    owners = [{"tm": (me - d + n) % n} for d in SEPARATIONS]
    greet(owners)
    copies = [
        remote(values_ref.at[pl.ds(o * slots, slots)], parts.at[o], send.at[o], recv.at[o], owner)
        for o, owner in enumerate(owners)
    ]
    for copy in copies:
        copy.start()
    for copy in copies:
        copy.wait()
    out_ref[0] = (parts[0] + parts[1]) + (parts[2] + parts[3])


def shards(n, layers, sources, sink, phase, task_table):
    ops, dim = sources.shape[1], sources.shape[-1]
    slots = task_table.shape[2]
    offsets = len(SEPARATIONS)
    third = 4
    steps = 2 * third if relays(n, layers) else 3 * third
    any_spec = pl.BlockSpec(memory_space=pl.ANY)
    smem_spec = pl.BlockSpec(memory_space=pltpu.SMEM)
    vmem_spec = pl.BlockSpec(memory_space=pltpu.VMEM)
    dma = pltpu.SemaphoreType.DMA
    limit = 60 * 1024 * 1024
    sinks, tables = pl.pallas_call(
        functools.partial(gather_kernel, n, layers, third),
        out_shape=(
            jax.ShapeDtypeStruct((offsets, 2 * dim, dim), sink.dtype),
            jax.ShapeDtypeStruct((offsets, 8, 128), jnp.int32),
        ),
        in_specs=[smem_spec, any_spec],
        out_specs=(any_spec, any_spec),
        scratch_shapes=[
            pltpu.VMEM((8, 128), jnp.int32),
            dma((offsets,)), dma((offsets,)),
            dma((steps,)), dma((steps,)), dma((steps,)), dma((steps,)),
            dma((third,)), dma((third,)), dma((third,)), dma((third,)),
            dma, dma, dma((3 * third,)), dma((3 * third,)),
        ],
        compiler_params=pltpu.CompilerParams(collective_id=0, has_side_effects=True, vmem_limit_bytes=limit),
        name="gather_sinks",
    )(task_table, sink.reshape(2 * dim, dim))
    values = pl.pallas_call(
        functools.partial(task_kernel, offsets, slots),
        out_shape=jax.ShapeDtypeStruct((offsets * slots + 1, 2, dim), jnp.float32),
        in_specs=[any_spec] * 4,
        out_specs=vmem_spec,
        scratch_shapes=[
            pltpu.VMEM((2, dim, 2 * dim), sources.dtype),
            pltpu.VMEM((2, 2 * dim, 2 * dim), sources.dtype),
            pltpu.VMEM((2, dim, 2 * dim), jnp.float32),
            pltpu.SMEM((offsets, 8, 128), jnp.int32),
            pltpu.VMEM(phase.shape, jnp.float32),
            pltpu.VMEM(phase.shape, jnp.float32),
            pltpu.VMEM(phase.shape, jnp.float32),
            pltpu.SMEM((offsets * slots,), jnp.int32),
            dma((2, 5)), dma((2,)),
        ],
        compiler_params=pltpu.CompilerParams(vmem_limit_bytes=limit),
        name="tasks",
    )(tables, phase, sources[0], sinks.reshape(offsets, 2, dim, dim))
    return pl.pallas_call(
        functools.partial(return_kernel, n),
        out_shape=jax.ShapeDtypeStruct((1, slots, 2, dim), jnp.float32),
        in_specs=[any_spec],
        out_specs=vmem_spec,
        scratch_shapes=[
            pltpu.VMEM((offsets, slots, 2, dim), jnp.float32),
            dma((offsets,)), dma((offsets,)),
        ],
        compiler_params=pltpu.CompilerParams(collective_id=1, has_side_effects=True, vmem_limit_bytes=limit),
        name="return_values",
    )(values)


def solution(mesh):
    return jax.shard_map(
        functools.partial(shards, mesh.shape["tm"], mesh.shape["op"]),
        mesh=mesh,
        in_specs=(
            P(("grp", "tm"), "op", None, None, None),
            P(("grp", "tm"), None, None, None),
            P(),
            P(None, ("grp", "tm"), "op"),
        ),
        out_specs=P(("grp", "tm"), "op", None, None),
        check_vma=False,
    )
```

```python
import functools

import jax
import jax.numpy as jnp
from jax import lax
from jax.experimental import pallas as pl
from jax.experimental.pallas import tpu as pltpu
from jax.sharding import PartitionSpec as P

SEPARATIONS = (-2, -1, 1, 2)
MESH = pl.DeviceIdType.MESH


def greet(neighbours):
    barrier = pltpu.get_barrier_semaphore()
    for neighbour in neighbours:
        pl.semaphore_signal(barrier, inc=1, device_id=neighbour, device_id_type=MESH)
    pl.semaphore_wait(barrier, len(neighbours))


def remote(src, dst, send, recv, neighbour):
    return pltpu.make_async_remote_copy(
        src_ref=src, dst_ref=dst, send_sem=send, recv_sem=recv,
        device_id=neighbour, device_id_type=MESH,
    )


def relays(n, layers):
    return n == 8 and layers % 2 == 0


def gather_kernel(
    n, layers, third, table_ref, sink_ref, sinks_ref, tables_ref,
    own, t_send, t_recv, x_send, x_recv, y_send, y_recv, zx_send, zx_recv, zy_send, zy_recv,
    p_send, p_recv, f_send, f_recv,
):
    me = lax.axis_index("tm")
    slots = table_ref.shape[2]
    chip, core = me // 2, me % 2
    mate = {"tm": chip * 2 + 1 - core}
    relay = relays(n, layers)
    neighbours = [{"tm": (me - d + n) % n} for d in SEPARATIONS]
    rows = sink_ref.shape[0] // (3 * third)

    def part(ref, k):
        return ref.at[pl.ds(pl.multiple_of(k * rows, rows), rows)]

    if relay:
        layer = lax.axis_index("op")
        parity = layer % 2
        across = {"tm": ((chip // 2) * 2 + 1 - chip % 2) * 2 + core}
        beside = {"tm": (me + n // 2) % n}
        above = {"op": layer + 1 - 2 * parity}
        greet(neighbours + [beside, above])
        mine = [third * (1 + parity) + j for j in range(third)] + list(range(third))
        others = [third * (2 - parity) + j for j in range(third)]
        x_here = 3 * (chip % 2)
        y_here = 3 - x_here
        x_copies = [
            remote(part(sink_ref, p), part(sinks_ref.at[y_here], p), x_send.at[k], x_recv.at[k], across)
            for k, p in enumerate(mine)
        ]
        y_copies = [
            remote(part(sinks_ref.at[x_here], p), part(sinks_ref.at[y_here], p), y_send.at[k], y_recv.at[k], beside)
            for k, p in enumerate(mine)
        ]
        zx_copies = [
            remote(part(sinks_ref.at[x_here], p), part(sinks_ref.at[x_here], p), zx_send.at[k], zx_recv.at[k], above)
            for k, p in enumerate(mine[:third])
        ]
        zy_copies = [
            remote(part(sinks_ref.at[y_here], p), part(sinks_ref.at[y_here], p), zy_send.at[k], zy_recv.at[k], above)
            for k, p in enumerate(mine[:third])
        ]
        order = mine + others
        x_forward = 3 * core == x_here
    else:
        greet(neighbours)
        order = list(range(3 * third))
        x_copies = [
            remote(part(sink_ref, p), part(sinks_ref.at[0], p), x_send.at[p], x_recv.at[p], neighbours[3])
            for p in order
        ]
        y_copies = [
            remote(part(sink_ref, p), part(sinks_ref.at[3], p), y_send.at[p], y_recv.at[p], neighbours[0])
            for p in order
        ]
        x_forward = core == 0
    p_copy = remote(sink_ref, sinks_ref.at[2 - core], p_send, p_recv, mate)
    f_copies = [
        remote(part(sinks_ref.at[3 * core], p), part(sinks_ref.at[1 + core], p), f_send.at[k], f_recv.at[k], mate)
        for k, p in enumerate(order)
    ]

    def forward(k, now):
        @pl.when(now)
        def _():
            f_copies[k].start()

    for copy in x_copies:
        copy.start()
    if not relay:
        for copy in y_copies:
            copy.start()

    row = lax.broadcasted_iota(jnp.int32, own.shape, 0)
    lane = lax.broadcasted_iota(jnp.int32, own.shape, 1)
    packed = jnp.zeros(own.shape, jnp.int32)
    for f in range(3):
        for s in range(slots):
            packed = jnp.where((row == f) & (lane == s), table_ref[f, 0, s], packed)
    own[...] = packed
    t_copies = [
        remote(own, tables_ref.at[o], t_send.at[o], t_recv.at[o], {"tm": (me + d + n) % n})
        for o, d in enumerate(SEPARATIONS)
    ]
    for copy in t_copies:
        copy.start()
    p_copy.start()

    steps, lag = len(x_copies), 2
    for k in range(steps + 2 * lag):
        if k < steps:
            x_copies[k].wait_recv()
            if relay:
                y_copies[k].start()
                if k < third:
                    zx_copies[k].start()
            forward(k, x_forward)
        if 0 <= k - lag < steps:
            y_copies[k - lag].wait_recv()
            if relay and k - lag < third:
                zy_copies[k - lag].start()
            forward(k - lag, jnp.logical_not(x_forward))
        if relay and 0 <= k - third - 1 < third:
            zx_copies[k - third - 1].wait_recv()
            forward(steps + k - third - 1, x_forward)
        if relay and 0 <= k - 2 * lag < third:
            zy_copies[k - 2 * lag].wait_recv()
            forward(steps + k - 2 * lag, jnp.logical_not(x_forward))
    for copy in t_copies:
        copy.wait()
    p_copy.wait()
    for copy in f_copies:
        copy.wait()
    for copy in x_copies + y_copies:
        copy.wait_send()
    if relay:
        for copy in zx_copies + zy_copies:
            copy.wait_send()


def task_kernel(
    offsets, slots, tables_hbm, phase_hbm, sources_ref, sinks_ref, out_ref,
    source, weight, loops, tables_ref, phase_ref, cosine, sine, todo, sems, begin,
):
    ops, dim = sources_ref.shape[0], source.shape[1]
    spare = offsets * slots
    first, last = pl.ds(0, dim), pl.ds(dim, dim)
    table_copy = pltpu.make_async_copy(tables_hbm, tables_ref, begin.at[0])
    phase_copy = pltpu.make_async_copy(phase_hbm, phase_ref, begin.at[1])
    table_copy.start()
    phase_copy.start()
    out_ref[...] = jnp.zeros_like(out_ref)
    table_copy.wait()

    def scan(j, count):
        o, s = j // slots, j % slots
        mine = (tables_ref[o, 2, s] >= 0) & (tables_ref[o, 0, s] // ops == o)
        todo[count] = j
        return count + mine.astype(jnp.int32)

    count = lax.fori_loop(0, offsets * slots, scan, jnp.int32(0))

    def copies(i):
        j, slot = todo[i], i % 2
        o, s = j // slots, j % slots
        a = tables_ref[o, 0, s] % ops
        pairs = (
            (sources_ref.at[a, 0], source.at[slot, :, first]),
            (sources_ref.at[a, 1], source.at[slot, :, last]),
            (sinks_ref.at[o, 0], weight.at[slot, first, first]),
            (sinks_ref.at[o, 0], weight.at[slot, last, last]),
            (sinks_ref.at[o, 1], weight.at[slot, first, last]),
        )
        return [pltpu.make_async_copy(a, b, sems.at[slot, q]) for q, (a, b) in enumerate(pairs)]

    @pl.when(count > 0)
    def _():
        for copy in copies(0):
            copy.start()

    phase_copy.wait()
    cosine[...] = jnp.cos(phase_ref[...])
    sine[...] = jnp.sin(phase_ref[...])

    def finish(slot, j):
        real, imag = loops[slot, :, :dim], loops[slot, :, dim:]
        real_t, imag_t = real.T, imag.T
        out_ref[j, 0:1] = jnp.sum(real * real_t - imag * imag_t, axis=0, keepdims=True) / dim
        out_ref[j, 1:2] = jnp.sum(real * imag_t + imag * real_t, axis=0, keepdims=True) / dim

    def step(i, before):
        slot = i % 2
        for copy in copies(i):
            copy.wait()

        @pl.when(i + 1 < count)
        def _():
            for copy in copies(i + 1):
                copy.start()

        j = todo[i]
        moment = tables_ref[j // slots, 1, j % slots]
        weight[slot, dim:, :dim] = -weight[slot, :dim, dim:]
        quark = jnp.dot(source[slot], weight[slot], preferred_element_type=jnp.float32)
        finish(1 - slot, before)
        c, z = cosine[pl.ds(moment, 1), :], sine[pl.ds(moment, 1), :]
        real, imag = quark[:, :dim], quark[:, dim:]
        phased = jnp.concatenate([real * c - imag * z, real * z + imag * c], axis=1).astype(jnp.bfloat16)
        loops[slot] = lax.dot_general(
            phased, weight[slot], (((1,), (1,)), ((), ())), preferred_element_type=jnp.float32
        )
        return j

    final = lax.fori_loop(0, count, step, jnp.int32(spare))

    @pl.when(count > 0)
    def _():
        finish((count - 1) % 2, final)


def return_kernel(n, values_ref, out_ref, parts, send, recv):
    me = lax.axis_index("tm")
    slots = out_ref.shape[1]
    owners = [{"tm": (me - d + n) % n} for d in SEPARATIONS]
    greet(owners)
    copies = [
        remote(values_ref.at[pl.ds(o * slots, slots)], parts.at[o], send.at[o], recv.at[o], owner)
        for o, owner in enumerate(owners)
    ]
    for copy in copies:
        copy.start()
    for copy in copies:
        copy.wait()
    out_ref[0] = (parts[0] + parts[1]) + (parts[2] + parts[3])


def shards(n, layers, sources, sink, phase, task_table):
    ops, dim = sources.shape[1], sources.shape[-1]
    slots = task_table.shape[2]
    offsets = len(SEPARATIONS)
    third = 2
    steps = 2 * third if relays(n, layers) else 3 * third
    any_spec = pl.BlockSpec(memory_space=pl.ANY)
    smem_spec = pl.BlockSpec(memory_space=pltpu.SMEM)
    vmem_spec = pl.BlockSpec(memory_space=pltpu.VMEM)
    dma = pltpu.SemaphoreType.DMA
    limit = 60 * 1024 * 1024
    sinks, tables = pl.pallas_call(
        functools.partial(gather_kernel, n, layers, third),
        out_shape=(
            jax.ShapeDtypeStruct((offsets, 2 * dim, dim), sink.dtype),
            jax.ShapeDtypeStruct((offsets, 8, 128), jnp.int32),
        ),
        in_specs=[smem_spec, any_spec],
        out_specs=(any_spec, any_spec),
        scratch_shapes=[
            pltpu.VMEM((8, 128), jnp.int32),
            dma((offsets,)), dma((offsets,)),
            dma((steps,)), dma((steps,)), dma((steps,)), dma((steps,)),
            dma((third,)), dma((third,)), dma((third,)), dma((third,)),
            dma, dma, dma((3 * third,)), dma((3 * third,)),
        ],
        compiler_params=pltpu.CompilerParams(collective_id=0, has_side_effects=True, vmem_limit_bytes=limit),
        name="gather_sinks",
    )(task_table, sink.reshape(2 * dim, dim))
    values = pl.pallas_call(
        functools.partial(task_kernel, offsets, slots),
        out_shape=jax.ShapeDtypeStruct((offsets * slots + 1, 2, dim), jnp.float32),
        in_specs=[any_spec] * 4,
        out_specs=vmem_spec,
        scratch_shapes=[
            pltpu.VMEM((2, dim, 2 * dim), sources.dtype),
            pltpu.VMEM((2, 2 * dim, 2 * dim), sources.dtype),
            pltpu.VMEM((2, dim, 2 * dim), jnp.float32),
            pltpu.SMEM((offsets, 8, 128), jnp.int32),
            pltpu.VMEM(phase.shape, jnp.float32),
            pltpu.VMEM(phase.shape, jnp.float32),
            pltpu.VMEM(phase.shape, jnp.float32),
            pltpu.SMEM((offsets * slots,), jnp.int32),
            dma((2, 5)), dma((2,)),
        ],
        compiler_params=pltpu.CompilerParams(vmem_limit_bytes=limit),
        name="tasks",
    )(tables, phase, sources[0], sinks.reshape(offsets, 2, dim, dim))
    return pl.pallas_call(
        functools.partial(return_kernel, n),
        out_shape=jax.ShapeDtypeStruct((1, slots, 2, dim), jnp.float32),
        in_specs=[any_spec],
        out_specs=vmem_spec,
        scratch_shapes=[
            pltpu.VMEM((offsets, slots, 2, dim), jnp.float32),
            dma((offsets,)), dma((offsets,)),
        ],
        compiler_params=pltpu.CompilerParams(collective_id=1, has_side_effects=True, vmem_limit_bytes=limit),
        name="return_values",
    )(values)


def solution(mesh):
    return jax.shard_map(
        functools.partial(shards, mesh.shape["tm"], mesh.shape["op"]),
        mesh=mesh,
        in_specs=(
            P(("grp", "tm"), "op", None, None, None),
            P(("grp", "tm"), None, None, None),
            P(),
            P(None, ("grp", "tm"), "op"),
        ),
        out_specs=P(("grp", "tm"), "op", None, None),
        check_vma=False,
    )
```

```python
import functools

import jax
import jax.numpy as jnp
from jax import lax
from jax.experimental import pallas as pl
from jax.experimental.pallas import tpu as pltpu
from jax.sharding import PartitionSpec as P

SEPARATIONS = (-2, -1, 1, 2)
MESH = pl.DeviceIdType.MESH


def greet(neighbours):
    barrier = pltpu.get_barrier_semaphore()
    for neighbour in neighbours:
        pl.semaphore_signal(barrier, inc=1, device_id=neighbour, device_id_type=MESH)
    pl.semaphore_wait(barrier, len(neighbours))


def remote(src, dst, send, recv, neighbour):
    return pltpu.make_async_remote_copy(
        src_ref=src, dst_ref=dst, send_sem=send, recv_sem=recv,
        device_id=neighbour, device_id_type=MESH,
    )


def relays(n, layers):
    return n == 8 and layers % 2 == 0


def gather_kernel(
    n, layers, third, table_ref, sink_ref, sinks_ref, tables_ref,
    own, t_send, t_recv, x_send, x_recv, y_send, y_recv, zx_send, zx_recv, zy_send, zy_recv,
    p_send, p_recv, f_send, f_recv,
):
    me = lax.axis_index("tm")
    slots = table_ref.shape[2]
    chip, core = me // 2, me % 2
    mate = {"tm": chip * 2 + 1 - core}
    relay = relays(n, layers)
    neighbours = [{"tm": (me - d + n) % n} for d in SEPARATIONS]
    rows = sink_ref.shape[0] // (3 * third)

    def part(ref, k):
        return ref.at[pl.ds(pl.multiple_of(k * rows, rows), rows)]

    if relay:
        layer = lax.axis_index("op")
        parity = layer % 2
        across = {"tm": ((chip // 2) * 2 + 1 - chip % 2) * 2 + core}
        beside = {"tm": (me + n // 2) % n}
        above = {"op": layer + 1 - 2 * parity}
        greet(neighbours + [beside, above])
        mine = [third * (1 + parity) + j for j in range(third)] + list(range(third))
        others = [third * (2 - parity) + j for j in range(third)]
        x_here = 3 * (chip % 2)
        y_here = 3 - x_here
        x_copies = [
            remote(part(sink_ref, p), part(sinks_ref.at[y_here], p), x_send.at[k], x_recv.at[k], across)
            for k, p in enumerate(mine)
        ]
        y_copies = [
            remote(part(sinks_ref.at[x_here], p), part(sinks_ref.at[y_here], p), y_send.at[k], y_recv.at[k], beside)
            for k, p in enumerate(mine)
        ]
        zx_copies = [
            remote(part(sinks_ref.at[x_here], p), part(sinks_ref.at[x_here], p), zx_send.at[k], zx_recv.at[k], above)
            for k, p in enumerate(mine[:third])
        ]
        zy_copies = [
            remote(part(sinks_ref.at[y_here], p), part(sinks_ref.at[y_here], p), zy_send.at[k], zy_recv.at[k], above)
            for k, p in enumerate(mine[:third])
        ]
        order = mine + others
        x_forward = 3 * core == x_here
    else:
        greet(neighbours)
        order = list(range(3 * third))
        x_copies = [
            remote(part(sink_ref, p), part(sinks_ref.at[0], p), x_send.at[p], x_recv.at[p], neighbours[3])
            for p in order
        ]
        y_copies = [
            remote(part(sink_ref, p), part(sinks_ref.at[3], p), y_send.at[p], y_recv.at[p], neighbours[0])
            for p in order
        ]
        x_forward = core == 0
    p_copy = remote(sink_ref, sinks_ref.at[2 - core], p_send, p_recv, mate)
    f_copies = [
        remote(part(sinks_ref.at[3 * core], p), part(sinks_ref.at[1 + core], p), f_send.at[k], f_recv.at[k], mate)
        for k, p in enumerate(order)
    ]

    def forward(k, now):
        @pl.when(now)
        def _():
            f_copies[k].start()

    for copy in x_copies:
        copy.start()
    if not relay:
        for copy in y_copies:
            copy.start()

    row = lax.broadcasted_iota(jnp.int32, own.shape, 0)
    lane = lax.broadcasted_iota(jnp.int32, own.shape, 1)
    packed = jnp.zeros(own.shape, jnp.int32)
    for f in range(3):
        for s in range(slots):
            packed = jnp.where((row == f) & (lane == s), table_ref[f, 0, s], packed)
    own[...] = packed
    t_copies = [
        remote(own, tables_ref.at[o], t_send.at[o], t_recv.at[o], {"tm": (me + d + n) % n})
        for o, d in enumerate(SEPARATIONS)
    ]
    for copy in t_copies:
        copy.start()
    p_copy.start()

    steps, lag = len(x_copies), 3
    for k in range(steps + 2 * lag):
        if k < steps:
            x_copies[k].wait_recv()
            if relay:
                y_copies[k].start()
                if k < third:
                    zx_copies[k].start()
            forward(k, x_forward)
        if 0 <= k - lag < steps:
            y_copies[k - lag].wait_recv()
            if relay and k - lag < third:
                zy_copies[k - lag].start()
            forward(k - lag, jnp.logical_not(x_forward))
        if relay and 0 <= k - third < third:
            zx_copies[k - third].wait_recv()
            forward(steps + k - third, x_forward)
        if relay and 0 <= k - 2 * lag < third:
            zy_copies[k - 2 * lag].wait_recv()
            forward(steps + k - 2 * lag, jnp.logical_not(x_forward))
    for copy in t_copies:
        copy.wait()
    p_copy.wait()
    for copy in f_copies:
        copy.wait()
    for copy in x_copies + y_copies:
        copy.wait_send()
    if relay:
        for copy in zx_copies + zy_copies:
            copy.wait_send()


def task_kernel(
    offsets, slots, tables_hbm, phase_hbm, sources_ref, sinks_ref, out_ref,
    source, weight, loops, tables_ref, phase_ref, cosine, sine, todo, sems, begin,
):
    ops, dim = sources_ref.shape[0], source.shape[1]
    spare = offsets * slots
    first, last = pl.ds(0, dim), pl.ds(dim, dim)
    table_copy = pltpu.make_async_copy(tables_hbm, tables_ref, begin.at[0])
    phase_copy = pltpu.make_async_copy(phase_hbm, phase_ref, begin.at[1])
    table_copy.start()
    phase_copy.start()
    out_ref[...] = jnp.zeros_like(out_ref)
    table_copy.wait()

    def scan(j, count):
        o, s = j // slots, j % slots
        mine = (tables_ref[o, 2, s] >= 0) & (tables_ref[o, 0, s] // ops == o)
        todo[count] = j
        return count + mine.astype(jnp.int32)

    count = lax.fori_loop(0, offsets * slots, scan, jnp.int32(0))

    def copies(i):
        j, slot = todo[i], i % 2
        o, s = j // slots, j % slots
        a = tables_ref[o, 0, s] % ops
        pairs = (
            (sources_ref.at[a, 0], source.at[slot, :, first]),
            (sources_ref.at[a, 1], source.at[slot, :, last]),
            (sinks_ref.at[o, 0], weight.at[slot, first, first]),
            (sinks_ref.at[o, 0], weight.at[slot, last, last]),
            (sinks_ref.at[o, 1], weight.at[slot, first, last]),
        )
        return [pltpu.make_async_copy(a, b, sems.at[slot, q]) for q, (a, b) in enumerate(pairs)]

    @pl.when(count > 0)
    def _():
        for copy in copies(0):
            copy.start()

    phase_copy.wait()
    cosine[...] = jnp.cos(phase_ref[...])
    sine[...] = jnp.sin(phase_ref[...])

    def finish(slot, j):
        real, imag = loops[slot, :, :dim], loops[slot, :, dim:]
        real_t, imag_t = real.T, imag.T
        out_ref[j, 0:1] = jnp.sum(real * real_t - imag * imag_t, axis=0, keepdims=True) / dim
        out_ref[j, 1:2] = jnp.sum(real * imag_t + imag * real_t, axis=0, keepdims=True) / dim

    def step(i, before):
        slot = i % 2
        for copy in copies(i):
            copy.wait()

        @pl.when(i + 1 < count)
        def _():
            for copy in copies(i + 1):
                copy.start()

        j = todo[i]
        moment = tables_ref[j // slots, 1, j % slots]
        weight[slot, dim:, :dim] = -weight[slot, :dim, dim:]
        quark = jnp.dot(source[slot], weight[slot], preferred_element_type=jnp.float32)
        finish(1 - slot, before)
        c, z = cosine[pl.ds(moment, 1), :], sine[pl.ds(moment, 1), :]
        real, imag = quark[:, :dim], quark[:, dim:]
        phased = jnp.concatenate([real * c - imag * z, real * z + imag * c], axis=1).astype(jnp.bfloat16)
        loops[slot] = lax.dot_general(
            phased, weight[slot], (((1,), (1,)), ((), ())), preferred_element_type=jnp.float32
        )
        return j

    final = lax.fori_loop(0, count, step, jnp.int32(spare))

    @pl.when(count > 0)
    def _():
        finish((count - 1) % 2, final)


def return_kernel(n, values_ref, out_ref, parts, send, recv):
    me = lax.axis_index("tm")
    slots = out_ref.shape[1]
    owners = [{"tm": (me - d + n) % n} for d in SEPARATIONS]
    greet(owners)
    copies = [
        remote(values_ref.at[pl.ds(o * slots, slots)], parts.at[o], send.at[o], recv.at[o], owner)
        for o, owner in enumerate(owners)
    ]
    for copy in copies:
        copy.start()
    for copy in copies:
        copy.wait()
    out_ref[0] = (parts[0] + parts[1]) + (parts[2] + parts[3])


def shards(n, layers, sources, sink, phase, task_table):
    ops, dim = sources.shape[1], sources.shape[-1]
    slots = task_table.shape[2]
    offsets = len(SEPARATIONS)
    third = 4
    steps = 2 * third if relays(n, layers) else 3 * third
    any_spec = pl.BlockSpec(memory_space=pl.ANY)
    smem_spec = pl.BlockSpec(memory_space=pltpu.SMEM)
    vmem_spec = pl.BlockSpec(memory_space=pltpu.VMEM)
    dma = pltpu.SemaphoreType.DMA
    limit = 60 * 1024 * 1024
    sinks, tables = pl.pallas_call(
        functools.partial(gather_kernel, n, layers, third),
        out_shape=(
            jax.ShapeDtypeStruct((offsets, 2 * dim, dim), sink.dtype),
            jax.ShapeDtypeStruct((offsets, 8, 128), jnp.int32),
        ),
        in_specs=[smem_spec, any_spec],
        out_specs=(vmem_spec, any_spec),
        scratch_shapes=[
            pltpu.VMEM((8, 128), jnp.int32),
            dma((offsets,)), dma((offsets,)),
            dma((steps,)), dma((steps,)), dma((steps,)), dma((steps,)),
            dma((third,)), dma((third,)), dma((third,)), dma((third,)),
            dma, dma, dma((3 * third,)), dma((3 * third,)),
        ],
        compiler_params=pltpu.CompilerParams(collective_id=0, has_side_effects=True, vmem_limit_bytes=limit),
        name="gather_sinks",
    )(task_table, sink.reshape(2 * dim, dim))
    values = pl.pallas_call(
        functools.partial(task_kernel, offsets, slots),
        out_shape=jax.ShapeDtypeStruct((offsets * slots + 1, 2, dim), jnp.float32),
        in_specs=[any_spec] * 4,
        out_specs=vmem_spec,
        scratch_shapes=[
            pltpu.VMEM((2, dim, 2 * dim), sources.dtype),
            pltpu.VMEM((2, 2 * dim, 2 * dim), sources.dtype),
            pltpu.VMEM((2, dim, 2 * dim), jnp.float32),
            pltpu.SMEM((offsets, 8, 128), jnp.int32),
            pltpu.VMEM(phase.shape, jnp.float32),
            pltpu.VMEM(phase.shape, jnp.float32),
            pltpu.VMEM(phase.shape, jnp.float32),
            pltpu.SMEM((offsets * slots,), jnp.int32),
            dma((2, 5)), dma((2,)),
        ],
        compiler_params=pltpu.CompilerParams(vmem_limit_bytes=limit),
        name="tasks",
    )(tables, phase, sources[0], sinks.reshape(offsets, 2, dim, dim))
    return pl.pallas_call(
        functools.partial(return_kernel, n),
        out_shape=jax.ShapeDtypeStruct((1, slots, 2, dim), jnp.float32),
        in_specs=[any_spec],
        out_specs=vmem_spec,
        scratch_shapes=[
            pltpu.VMEM((offsets, slots, 2, dim), jnp.float32),
            dma((offsets,)), dma((offsets,)),
        ],
        compiler_params=pltpu.CompilerParams(collective_id=1, has_side_effects=True, vmem_limit_bytes=limit),
        name="return_values",
    )(values)


def solution(mesh):
    return jax.shard_map(
        functools.partial(shards, mesh.shape["tm"], mesh.shape["op"]),
        mesh=mesh,
        in_specs=(
            P(("grp", "tm"), "op", None, None, None),
            P(("grp", "tm"), None, None, None),
            P(),
            P(None, ("grp", "tm"), "op"),
        ),
        out_specs=P(("grp", "tm"), "op", None, None),
        check_vma=False,
    )
```

```python
import functools

import jax
import jax.numpy as jnp
from jax import lax
from jax.experimental import pallas as pl
from jax.experimental.pallas import tpu as pltpu
from jax.sharding import PartitionSpec as P

SEPARATIONS = (-2, -1, 1, 2)
MESH = pl.DeviceIdType.MESH


def greet(neighbours):
    barrier = pltpu.get_barrier_semaphore()
    for neighbour in neighbours:
        pl.semaphore_signal(barrier, inc=1, device_id=neighbour, device_id_type=MESH)
    pl.semaphore_wait(barrier, len(neighbours))


def remote(src, dst, send, recv, neighbour):
    return pltpu.make_async_remote_copy(
        src_ref=src, dst_ref=dst, send_sem=send, recv_sem=recv,
        device_id=neighbour, device_id_type=MESH,
    )


def relays(n, layers):
    return n == 8 and layers % 2 == 0


def gather_kernel(
    n, layers, third, table_ref, sink_ref, sinks_ref, tables_ref,
    own, t_send, t_recv, x_send, x_recv, y_send, y_recv, zx_send, zx_recv, zy_send, zy_recv,
    p_send, p_recv, f_send, f_recv,
):
    me = lax.axis_index("tm")
    slots = table_ref.shape[2]
    chip, core = me // 2, me % 2
    mate = {"tm": chip * 2 + 1 - core}
    relay = relays(n, layers)
    neighbours = [{"tm": (me - d + n) % n} for d in SEPARATIONS]
    rows = sink_ref.shape[0] // (3 * third)

    def part(ref, k):
        return ref.at[pl.ds(pl.multiple_of(k * rows, rows), rows)]

    if relay:
        layer = lax.axis_index("op")
        parity = layer % 2
        across = {"tm": ((chip // 2) * 2 + 1 - chip % 2) * 2 + core}
        beside = {"tm": (me + n // 2) % n}
        above = {"op": layer + 1 - 2 * parity}
        greet(neighbours + [beside, above])
        mine = [third * (1 + parity) + j for j in range(third)] + list(range(third))
        others = [third * (2 - parity) + j for j in range(third)]
        x_here = 3 * (chip % 2)
        y_here = 3 - x_here
        x_copies = [
            remote(part(sink_ref, p), part(sinks_ref.at[y_here], p), x_send.at[k], x_recv.at[k], across)
            for k, p in enumerate(mine)
        ]
        y_copies = [
            remote(part(sinks_ref.at[x_here], p), part(sinks_ref.at[y_here], p), y_send.at[k], y_recv.at[k], beside)
            for k, p in enumerate(mine)
        ]
        zx_copies = [
            remote(part(sinks_ref.at[x_here], p), part(sinks_ref.at[x_here], p), zx_send.at[k], zx_recv.at[k], above)
            for k, p in enumerate(mine[:third])
        ]
        zy_copies = [
            remote(part(sinks_ref.at[y_here], p), part(sinks_ref.at[y_here], p), zy_send.at[k], zy_recv.at[k], above)
            for k, p in enumerate(mine[:third])
        ]
        order = mine + others
        x_forward = 3 * core == x_here
    else:
        greet(neighbours)
        order = list(range(3 * third))
        x_copies = [
            remote(part(sink_ref, p), part(sinks_ref.at[0], p), x_send.at[p], x_recv.at[p], neighbours[3])
            for p in order
        ]
        y_copies = [
            remote(part(sink_ref, p), part(sinks_ref.at[3], p), y_send.at[p], y_recv.at[p], neighbours[0])
            for p in order
        ]
        x_forward = core == 0
    p_copy = remote(sink_ref, sinks_ref.at[2 - core], p_send, p_recv, mate)
    f_copies = [
        remote(part(sinks_ref.at[3 * core], p), part(sinks_ref.at[1 + core], p), f_send.at[k], f_recv.at[k], mate)
        for k, p in enumerate(order)
    ]

    def forward(k, now):
        @pl.when(now)
        def _():
            f_copies[k].start()

    for copy in x_copies:
        copy.start()
    if not relay:
        for copy in y_copies:
            copy.start()

    row = lax.broadcasted_iota(jnp.int32, own.shape, 0)
    lane = lax.broadcasted_iota(jnp.int32, own.shape, 1)
    packed = jnp.zeros(own.shape, jnp.int32)
    for f in range(3):
        for s in range(slots):
            packed = jnp.where((row == f) & (lane == s), table_ref[f, 0, s], packed)
    own[...] = packed
    t_copies = [
        remote(own, tables_ref.at[o], t_send.at[o], t_recv.at[o], {"tm": (me + d + n) % n})
        for o, d in enumerate(SEPARATIONS)
    ]
    for copy in t_copies:
        copy.start()
    p_copy.start()

    steps, lag = len(x_copies), 5
    for k in range(steps + 2 * lag):
        if k < steps:
            x_copies[k].wait_recv()
            if relay:
                y_copies[k].start()
                if k < third:
                    zx_copies[k].start()
            forward(k, x_forward)
        if 0 <= k - lag < steps:
            y_copies[k - lag].wait_recv()
            if relay and k - lag < third:
                zy_copies[k - lag].start()
            forward(k - lag, jnp.logical_not(x_forward))
        if relay and 0 <= k - third < third:
            zx_copies[k - third].wait_recv()
            forward(steps + k - third, x_forward)
        if relay and 0 <= k - 2 * lag < third:
            zy_copies[k - 2 * lag].wait_recv()
            forward(steps + k - 2 * lag, jnp.logical_not(x_forward))
    for copy in t_copies:
        copy.wait()
    p_copy.wait()
    for copy in f_copies:
        copy.wait()
    for copy in x_copies + y_copies:
        copy.wait_send()
    if relay:
        for copy in zx_copies + zy_copies:
            copy.wait_send()


def task_kernel(
    offsets, slots, tables_hbm, phase_hbm, sources_ref, sinks_ref, out_ref,
    source, weight, loops, tables_ref, phase_ref, cosine, sine, todo, sems, begin,
):
    ops, dim = sources_ref.shape[0], source.shape[1]
    spare = offsets * slots
    first, last = pl.ds(0, dim), pl.ds(dim, dim)
    table_copy = pltpu.make_async_copy(tables_hbm, tables_ref, begin.at[0])
    phase_copy = pltpu.make_async_copy(phase_hbm, phase_ref, begin.at[1])
    table_copy.start()
    phase_copy.start()
    out_ref[...] = jnp.zeros_like(out_ref)
    table_copy.wait()

    def scan(j, count):
        o, s = j // slots, j % slots
        mine = (tables_ref[o, 2, s] >= 0) & (tables_ref[o, 0, s] // ops == o)
        todo[count] = j
        return count + mine.astype(jnp.int32)

    count = lax.fori_loop(0, offsets * slots, scan, jnp.int32(0))

    def copies(i):
        j, slot = todo[i], i % 2
        o, s = j // slots, j % slots
        a = tables_ref[o, 0, s] % ops
        pairs = (
            (sources_ref.at[a, 0], source.at[slot, :, first]),
            (sources_ref.at[a, 1], source.at[slot, :, last]),
            (sinks_ref.at[o, 0], weight.at[slot, first, first]),
            (sinks_ref.at[o, 0], weight.at[slot, last, last]),
            (sinks_ref.at[o, 1], weight.at[slot, first, last]),
        )
        return [pltpu.make_async_copy(a, b, sems.at[slot, q]) for q, (a, b) in enumerate(pairs)]

    @pl.when(count > 0)
    def _():
        for copy in copies(0):
            copy.start()

    phase_copy.wait()
    cosine[...] = jnp.cos(phase_ref[...])
    sine[...] = jnp.sin(phase_ref[...])

    def finish(slot, j):
        real, imag = loops[slot, :, :dim], loops[slot, :, dim:]
        real_t, imag_t = real.T, imag.T
        out_ref[j, 0:1] = jnp.sum(real * real_t - imag * imag_t, axis=0, keepdims=True) / dim
        out_ref[j, 1:2] = jnp.sum(real * imag_t + imag * real_t, axis=0, keepdims=True) / dim

    def step(i, before):
        slot = i % 2
        for copy in copies(i):
            copy.wait()

        @pl.when(i + 1 < count)
        def _():
            for copy in copies(i + 1):
                copy.start()

        j = todo[i]
        moment = tables_ref[j // slots, 1, j % slots]
        weight[slot, dim:, :dim] = -weight[slot, :dim, dim:]
        quark = jnp.dot(source[slot], weight[slot], preferred_element_type=jnp.float32)
        finish(1 - slot, before)
        c, z = cosine[pl.ds(moment, 1), :], sine[pl.ds(moment, 1), :]
        real, imag = quark[:, :dim], quark[:, dim:]
        phased = jnp.concatenate([real * c - imag * z, real * z + imag * c], axis=1).astype(jnp.bfloat16)
        loops[slot] = lax.dot_general(
            phased, weight[slot], (((1,), (1,)), ((), ())), preferred_element_type=jnp.float32
        )
        return j

    final = lax.fori_loop(0, count, step, jnp.int32(spare))

    @pl.when(count > 0)
    def _():
        finish((count - 1) % 2, final)


def return_kernel(n, values_ref, out_ref, parts, send, recv):
    me = lax.axis_index("tm")
    slots = out_ref.shape[1]
    owners = [{"tm": (me - d + n) % n} for d in SEPARATIONS]
    greet(owners)
    copies = [
        remote(values_ref.at[pl.ds(o * slots, slots)], parts.at[o], send.at[o], recv.at[o], owner)
        for o, owner in enumerate(owners)
    ]
    for copy in copies:
        copy.start()
    for copy in copies:
        copy.wait()
    out_ref[0] = (parts[0] + parts[1]) + (parts[2] + parts[3])


def shards(n, layers, sources, sink, phase, task_table):
    ops, dim = sources.shape[1], sources.shape[-1]
    slots = task_table.shape[2]
    offsets = len(SEPARATIONS)
    third = 4
    steps = 2 * third if relays(n, layers) else 3 * third
    any_spec = pl.BlockSpec(memory_space=pl.ANY)
    smem_spec = pl.BlockSpec(memory_space=pltpu.SMEM)
    vmem_spec = pl.BlockSpec(memory_space=pltpu.VMEM)
    dma = pltpu.SemaphoreType.DMA
    limit = 60 * 1024 * 1024
    sinks, tables = pl.pallas_call(
        functools.partial(gather_kernel, n, layers, third),
        out_shape=(
            jax.ShapeDtypeStruct((offsets, 2 * dim, dim), sink.dtype),
            jax.ShapeDtypeStruct((offsets, 8, 128), jnp.int32),
        ),
        in_specs=[smem_spec, any_spec],
        out_specs=(any_spec, any_spec),
        scratch_shapes=[
            pltpu.VMEM((8, 128), jnp.int32),
            dma((offsets,)), dma((offsets,)),
            dma((steps,)), dma((steps,)), dma((steps,)), dma((steps,)),
            dma((third,)), dma((third,)), dma((third,)), dma((third,)),
            dma, dma, dma((3 * third,)), dma((3 * third,)),
        ],
        compiler_params=pltpu.CompilerParams(collective_id=0, has_side_effects=True, vmem_limit_bytes=limit),
        name="gather_sinks",
    )(task_table, sink.reshape(2 * dim, dim))
    values = pl.pallas_call(
        functools.partial(task_kernel, offsets, slots),
        out_shape=jax.ShapeDtypeStruct((offsets * slots + 1, 2, dim), jnp.float32),
        in_specs=[any_spec] * 4,
        out_specs=vmem_spec,
        scratch_shapes=[
            pltpu.VMEM((2, dim, 2 * dim), sources.dtype),
            pltpu.VMEM((2, 2 * dim, 2 * dim), sources.dtype),
            pltpu.VMEM((2, dim, 2 * dim), jnp.float32),
            pltpu.SMEM((offsets, 8, 128), jnp.int32),
            pltpu.VMEM(phase.shape, jnp.float32),
            pltpu.VMEM(phase.shape, jnp.float32),
            pltpu.VMEM(phase.shape, jnp.float32),
            pltpu.SMEM((offsets * slots,), jnp.int32),
            dma((2, 5)), dma((2,)),
        ],
        compiler_params=pltpu.CompilerParams(vmem_limit_bytes=limit),
        name="tasks",
    )(tables, phase, sources[0], sinks.reshape(offsets, 2, dim, dim))
    return pl.pallas_call(
        functools.partial(return_kernel, n),
        out_shape=jax.ShapeDtypeStruct((1, slots, 2, dim), jnp.float32),
        in_specs=[any_spec],
        out_specs=vmem_spec,
        scratch_shapes=[
            pltpu.VMEM((offsets, slots, 2, dim), jnp.float32),
            dma((offsets,)), dma((offsets,)),
        ],
        compiler_params=pltpu.CompilerParams(collective_id=1, has_side_effects=True, vmem_limit_bytes=limit),
        name="return_values",
    )(values)


def solution(mesh):
    return jax.shard_map(
        functools.partial(shards, mesh.shape["tm"], mesh.shape["op"]),
        mesh=mesh,
        in_specs=(
            P(("grp", "tm"), "op", None, None, None),
            P(("grp", "tm"), None, None, None),
            P(),
            P(None, ("grp", "tm"), "op"),
        ),
        out_specs=P(("grp", "tm"), "op", None, None),
        check_vma=False,
    )
```
